256 devices in a mesh: ctx: 8 (over y, core), head: 32 (over x, z).
Axes of the slice: x: 4, y: 4, z: 8, core: 2. Of those that a mesh axis runs over, the one named last changes fastest.
Arguments:
- queries: bfloat16 [32768, 4096], P('ctx', 'head'), may hold values from -24 to 24
- win_key: bfloat16 [32768, 1024], P(('ctx', 'head')), may hold values from -24 to 24
- win_value: bfloat16 [32768, 1024], P(('ctx', 'head')), may hold values from -6 to 6
- past_key: bfloat16 [524288, 1024], P(('ctx', 'head')), may hold values from -24 to 24
- past_value: bfloat16 [524288, 1024], P(('ctx', 'head')), may hold values from -6 to 6
- chosen: int32 [256, 32, 3], P('ctx', 'head'), may hold values from 0 to 1023, as said below
Outputs:
- attended: bfloat16 [32768, 4096], P('ctx', 'head')
The draws below stay inside these ranges and needn't reach their ends.
Inputs may be any that keep to these rules, and one draw needn't show every extreme that they name: `chosen`: block b of the cache is held by the device of linear index b // 4, counted over ctx then head. Of the entries held by one device (its query blocks and its heads), at most 1 fall on any one owner, and one owner receives exactly 1 from every device. The 3 blocks of one list lie on distinct owners.
All inputs are finite; a program needn't handle non-finite values.
Results may differ from the reference program's by a relative error of at most 0.019.
Values may be sent and summed in bfloat16 or wider, within the bound.
No kernel may reach another device: no remote copies, remote signals or barrier semaphores. Data moves between devices by JAX's collectives and lax.ppermute only.
A program may use at most 128 MiB of HBM per device.

```python
import math
import jax
import jax.numpy as jnp
from jax import lax

HEADS = 32
KVH = 8
DH = 128
BLK = 512
QBLK = 128
TOPK = 3
WINDOW = 32768
PAST = 524288
NBLOCKS = 1024
BLK_DEV = 4
QB_DEV = 32
QBLOCKS = 256
HEAD_DEV = 1
REQ = 96
CAP = 1
N_CTX = 8
N_HEAD = 32
DEVICES = 256


def chosen_ids(key):
    key = jax.random.fold_in(key, 3)
    contender_count = DEVICES * CAP
    hot_order = jax.random.permutation(jax.random.fold_in(key, 1), DEVICES)
    holder_position = jnp.zeros((DEVICES,), jnp.int32).at[hot_order].set(jnp.arange(DEVICES, dtype=jnp.int32))
    popular_count = max(1, DEVICES // 16)
    holder_reward = jnp.where(holder_position == 0, 8192, jnp.where(holder_position <= popular_count, 4096, 0)).astype(jnp.int32)
    contender_holder = jnp.arange(contender_count, dtype=jnp.int32) // CAP
    jitter_sample = jax.random.randint(jax.random.fold_in(key, 2), (DEVICES, contender_count), 0, 4096, jnp.int32)
    contender_scores = (jitter_sample + holder_reward[contender_holder][None, :]) * contender_count + jnp.arange(contender_count, dtype=jnp.int32)[None, :]
    top_values, top_index = lax.top_k(contender_scores, REQ)
    ordered = jnp.sort(top_index, axis=1)
    owners = ordered // CAP
    lists_dev = QB_DEV * HEAD_DEV
    spread = owners.reshape(DEVICES, TOPK, lists_dev).transpose(0, 2, 1)
    shuffle_keys = jax.random.randint(jax.random.fold_in(key, 3), (DEVICES, lists_dev, TOPK), 0, 65536, jnp.int32) * TOPK + jnp.arange(TOPK, dtype=jnp.int32)
    shuffle_order = jnp.argsort(shuffle_keys, axis=-1)
    spread = jnp.take_along_axis(spread, shuffle_order, axis=-1)
    offsets = jax.random.randint(jax.random.fold_in(key, 4), (DEVICES, lists_dev, TOPK), 0, BLK_DEV, jnp.int32)
    block_ids = spread * BLK_DEV + offsets
    block_ids = block_ids.reshape(N_CTX, N_HEAD, QB_DEV, HEAD_DEV, TOPK).transpose(0, 2, 1, 3, 4)
    return block_ids.reshape(QBLOCKS, HEADS, TOPK).astype(jnp.int32)


def draw_queries(key, part):
    key = jax.random.fold_in(key, 1)
    base_values = jax.random.normal(key, (WINDOW, HEADS, DH), jnp.float32)
    values = jnp.clip(base_values, -6.0, 6.0)
    return values.reshape(WINDOW, HEADS * DH).astype(jnp.bfloat16)


def draw_win_key(key, part):
    key = jax.random.fold_in(key, 2)
    base_values = jax.random.normal(key, (WINDOW, KVH, DH), jnp.float32)
    values = jnp.clip(base_values, -6.0, 6.0)
    return values.reshape(WINDOW, KVH * DH).astype(jnp.bfloat16)


def draw_past_key(key, part):
    key = jax.random.fold_in(key, 4)
    base_values = jax.random.normal(key, (PAST, KVH, DH), jnp.float32)
    values = jnp.clip(base_values, -6.0, 6.0)
    return values.reshape(PAST, KVH * DH).astype(jnp.bfloat16)


def draw_chosen(key, part):
    return chosen_ids(key)


def steps_of(key, shape, cuts, smallest, top_value):
    factor_of, own = 1.0, jax.random.fold_in(key, 6)
    for position, blocks in cuts:
        heights = jnp.exp(jax.random.uniform(jax.random.fold_in(own, position), (blocks,), jnp.float32, smallest / len(cuts), top_value / len(cuts)))
        factor_of = factor_of * jnp.repeat(heights, shape[position] // blocks).reshape([-1 if axis == position else 1 for axis in range(len(shape))])
    return factor_of


def bell_draw(stream_key, dims, scale, bound, split=(), kind=jnp.bfloat16):
    loudness = steps_of(stream_key, dims, split, -0.22, 0.18) if split else 1.0
    drawn = jax.random.normal(stream_key, dims, jnp.float32) * scale * loudness
    return jnp.minimum(jnp.maximum(drawn, -bound), bound).astype(kind)


def setup_inputs(seed: int = 0) -> dict:
    key_list = jax.random.split(jax.random.key(seed), 7)
    queries = draw_queries(jax.random.fold_in(key_list[6], 71), 0)
    win_key = draw_win_key(jax.random.fold_in(key_list[6], 71), 0)
    win_value = bell_draw(key_list[2], (WINDOW, KVH * DH), 1.0, 6.0, ((0, 256),))
    past_key = draw_past_key(jax.random.fold_in(key_list[6], 71), 0)
    past_value = bell_draw(key_list[4], (PAST, KVH * DH), 1.0, 6.0, ((0, 256),))
    chosen = draw_chosen(jax.random.fold_in(key_list[6], 71), 0)
    return {"queries": queries, "win_key": win_key, "win_value": win_value, "past_key": past_key, "past_value": past_value, "chosen": chosen}


def reference(queries, win_key, win_value, past_key, past_value, chosen):
    scale_factor = 1.0 / math.sqrt(DH)
    group_size = HEADS // KVH
    window_blocks = WINDOW // BLK
    sub_blocks = BLK // QBLK
    query_stack = queries.reshape(window_blocks, BLK, HEADS, DH)
    wkey_stack = win_key.reshape(window_blocks, BLK, KVH, DH)
    wvalue_stack = win_value.reshape(window_blocks, BLK, KVH, DH)
    chosen_stack = chosen.reshape(window_blocks, sub_blocks, HEADS, TOPK)
    past_keys = past_key.reshape(NBLOCKS, BLK, KVH, DH)
    past_values = past_value.reshape(NBLOCKS, BLK, KVH, DH)
    head_to_kv = (jnp.arange(HEADS) // group_size).astype(jnp.int32)
    positions = jnp.arange(BLK)
    causal = positions[None, :] <= positions[:, None]

    def one_block(operands):
        query_block, wkey_block, wvalue_block, chosen_block = operands
        query_wide = query_block.astype(jnp.float32)
        wkey_heads = jnp.repeat(wkey_block, group_size, axis=1).astype(jnp.float32)
        wvalue_heads = jnp.repeat(wvalue_block, group_size, axis=1).astype(jnp.float32)
        own_scores = jnp.einsum('ihd,thd->hit', query_wide, wkey_heads) * scale_factor
        own_scores = jnp.where(causal[None], own_scores, -jnp.inf)
        own_max = lax.optimization_barrier(jnp.max(own_scores, axis=-1))
        own_terms = jnp.exp(own_scores - own_max[..., None])
        own_total = lax.optimization_barrier(jnp.sum(own_terms, axis=-1))
        own_rounded = lax.optimization_barrier(own_terms.astype(jnp.bfloat16)).astype(jnp.float32)
        own_out = jnp.einsum('hit,thd->hid', own_rounded, wvalue_heads)
        key_tiles = past_keys[chosen_block, :, head_to_kv[None, :, None], :].astype(jnp.float32)
        value_tiles = past_values[chosen_block, :, head_to_kv[None, :, None], :].astype(jnp.float32)
        query_tiles = query_wide.reshape(sub_blocks, QBLK, HEADS, DH)
        far_scores = jnp.einsum('aihd,ahktd->ahkit', query_tiles, key_tiles) * scale_factor
        far_max = lax.optimization_barrier(jnp.max(far_scores, axis=-1))
        far_terms = jnp.exp(far_scores - far_max[..., None])
        far_total = lax.optimization_barrier(jnp.sum(far_terms, axis=-1))
        far_rounded = lax.optimization_barrier(far_terms.astype(jnp.bfloat16)).astype(jnp.float32)
        far_out = jnp.einsum('ahkit,ahktd->ahkid', far_rounded, value_tiles)
        far_out = lax.optimization_barrier(far_out.astype(jnp.bfloat16)).astype(jnp.float32)
        own_max_t = own_max.reshape(HEADS, sub_blocks, QBLK).transpose(1, 0, 2)
        own_total_t = own_total.reshape(HEADS, sub_blocks, QBLK).transpose(1, 0, 2)
        own_out_t = own_out.reshape(HEADS, sub_blocks, QBLK, DH).transpose(1, 0, 2, 3)
        top_score = jnp.maximum(own_max_t, lax.optimization_barrier(jnp.max(far_max, axis=2)))
        own_weight = jnp.exp(own_max_t - top_score)
        far_weight = jnp.exp(far_max - top_score[:, :, None])
        total_weight = own_total_t * own_weight + lax.optimization_barrier(jnp.sum(far_total * far_weight, axis=2))
        numerator = own_out_t * own_weight[..., None] + lax.optimization_barrier(jnp.sum(far_out * far_weight[..., None], axis=2))
        merged = numerator / total_weight[..., None]
        return merged.transpose(0, 2, 1, 3).reshape(BLK, HEADS * DH).astype(jnp.bfloat16)
    result = lax.map(one_block, (query_stack, wkey_stack, wvalue_stack, chosen_stack))
    return result.reshape(WINDOW, HEADS * DH)
```

```python
import functools
import math

import jax
import jax.numpy as jnp
from jax import lax
from jax.experimental import pallas as pl
from jax.experimental.pallas import tpu as pltpu
from jax.sharding import Mesh, PartitionSpec as P

DH = 128
BLK = 512
QBLK = 128
TOPK = 3
TILES = 32
PLANE = 32
NZ = 8
REQ = 96
UNROLL = 4
EXP_SCALE = math.log2(math.e) / math.sqrt(DH)
NONE = -1e30
BF = jnp.bfloat16
F32 = jnp.float32

VMEM = pl.BlockSpec(memory_space=pltpu.VMEM)
SMEM = pl.BlockSpec(memory_space=pltpu.SMEM)
ANY = pl.BlockSpec(memory_space=pl.ANY)


def params():
    return pltpu.CompilerParams(vmem_limit_bytes=48 * 1024 * 1024)


def mxu(a, b):
    return jnp.dot(a, b, preferred_element_type=F32)


def pack_kernel(aways, stride, idx_ref, *refs):
    n = len(aways)
    sources, out_ref, sem = refs[:n], refs[n], refs[n + 1]

    @pl.loop(0, PLANE)
    def _(owner):
        for j in range(n):
            pltpu.make_async_copy(
                sources[j].at[idx_ref[owner * stride + aways[j]]],
                out_ref.at[owner, pl.ds(j * QBLK, QBLK), :],
                sem,
            ).start()

    pltpu.make_async_copy(out_ref, out_ref, sem).wait()


def pack(sources, aways, idx):
    stride = idx.shape[0] // PLANE
    n = len(sources)
    return pl.pallas_call(
        functools.partial(pack_kernel, aways, stride),
        out_shape=jax.ShapeDtypeStruct((PLANE, n * QBLK, DH), BF),
        in_specs=[SMEM] + [VMEM] * n,
        out_specs=ANY,
        scratch_shapes=[pltpu.SemaphoreType.DMA],
        compiler_params=params(),
        cost_estimate=pl.CostEstimate(
            flops=0, bytes_accessed=2 * n * PLANE * QBLK * DH * 2, transcendentals=0
        ),
        name=f"pack{n}",
    )(idx, *sources)


def far_kernel(
    aways, first, meta_ref, got_ref, k_ref, vt_ref, out_ref, q_ref, lse_ref, list_ref, sem
):
    n = len(aways)
    slots = PLANE * n

    def meta_of(slot):
        if n == 1:
            return meta_ref[slot * NZ + aways[0]]
        return meta_ref[slot // 2 * NZ + jnp.where(slot % 2 == 0, aways[0], aways[1])]

    copy = pltpu.make_async_copy(
        got_ref.at[:, first * QBLK : (first + n) * QBLK, :], q_ref, sem
    )
    copy.start()
    out_ref[...] = jnp.zeros_like(out_ref)
    lse_ref[...] = jnp.zeros_like(lse_ref)

    def listed(i, count):
        list_ref[count] = i
        return count + (meta_of(i) >= 0).astype(jnp.int32)

    count = lax.fori_loop(0, slots, listed, jnp.int32(0))
    last = list_ref[jnp.maximum(count - 1, 0)]
    for u in range(UNROLL):
        list_ref[count + u] = last
    copy.wait()

    @pl.loop(0, (count + UNROLL - 1) // UNROLL)
    def _(turn):
        ids = [list_ref[turn * UNROLL + u] for u in range(UNROLL)]
        scores, values = [], []
        for slot in ids:
            meta = meta_of(slot)
            keys = pl.multiple_of((meta // 8) * BLK, BLK)
            cols = pl.multiple_of((meta % 8) * DH, DH)
            q = q_ref[slot // n, pl.ds(pl.multiple_of(slot % n * QBLK, QBLK), QBLK), :]
            scores.append(mxu(k_ref[pl.ds(keys, BLK), pl.ds(cols, DH)], q))
            values.append(vt_ref[pl.ds(cols, DH), pl.ds(keys, BLK)])
        tops = [jnp.max(s, axis=0, keepdims=True) for s in scores]
        terms = [jnp.exp2((s - m) * EXP_SCALE) for s, m in zip(scores, tops)]
        totals = [jnp.sum(t, axis=0, keepdims=True) for t in terms]
        outs = [mxu(v, t.astype(BF)) for v, t in zip(values, terms)]
        for slot, o, m, l in zip(ids, outs, tops, totals):
            out_ref[slot // n, pl.ds(pl.multiple_of(slot % n * QBLK, QBLK), QBLK), :] = (
                o * (1.0 / l)
            ).astype(BF)
            lse_ref[slot] = m * EXP_SCALE + jnp.log2(l)

    @pl.loop(0, PLANE)
    def _(source):
        rows = []
        for j in range(n):
            rows += split3(lse_ref[source * n + j])
        rows.append(jnp.zeros((16 - len(rows), DH), F32))
        out_ref[source, n * QBLK :, :] = jnp.concatenate(rows, axis=0).astype(BF)


def far(tiles, first, aways, meta, past_key, past_value_t):
    n = len(aways)
    slots = PLANE * n
    return pl.pallas_call(
        functools.partial(far_kernel, aways, first),
        out_shape=jax.ShapeDtypeStruct((PLANE, n * QBLK + 16, DH), BF),
        in_specs=[SMEM, ANY, VMEM, VMEM],
        out_specs=VMEM,
        scratch_shapes=[
            pltpu.VMEM((PLANE, n * QBLK, DH), BF),
            pltpu.VMEM((slots, 1, DH), F32),
            pltpu.SMEM((slots + UNROLL,), jnp.int32),
            pltpu.SemaphoreType.DMA,
        ],
        compiler_params=params(),
        cost_estimate=pl.CostEstimate(
            flops=slots * 4 * QBLK * BLK * DH,
            bytes_accessed=12 * 2**20,
            transcendentals=slots * QBLK * BLK,
        ),
        name=f"far{n}",
    )(meta, tiles, past_key, past_value_t)


def own_kernel(aways, info_ref, kv_ref, *refs):
    n = len(aways)
    queries, out_ref, lse_ref = refs[:n], refs[n], refs[n + 1]
    z, column = info_ref[0], info_ref[1]
    half, part = z // 4, z % 4
    key_at = lax.broadcasted_iota(jnp.int32, (QBLK, QBLK), 0)
    row_at = lax.broadcasted_iota(jnp.int32, (QBLK, QBLK), 1)
    for j in range(n):
        group = (z + aways[j]) % NZ // 4

        @pl.loop(0, 4)
        def _(b):
            keys = kv_ref[b, group]
            values = kv_ref[b, 2 + group]
            block = (column - b + 4) % 4
            first = (block * 2 + half) * 4
            scores = [mxu(keys, queries[j][first + t]) for t in range(4)]
            scores = [
                jnp.where(key_at <= row_at + (t - part) * QBLK, s, NONE)
                for t, s in enumerate(scores)
            ]
            tops = [jnp.max(s, axis=0, keepdims=True) for s in scores]
            terms = [jnp.exp2((s - m) * EXP_SCALE) for s, m in zip(scores, tops)]
            totals = [jnp.sum(t, axis=0, keepdims=True) for t in terms]
            outs = [mxu(values, t.astype(BF)) for t in terms]
            sums = []
            for t in range(4):
                out_ref[j * 16 + block * 4 + t] = (outs[t] * (1.0 / totals[t])).astype(BF)
                x = tops[t] * EXP_SCALE + jnp.log2(totals[t])
                sums.append(x + jnp.where(part > t, NONE, 0.0))
            lse_ref[j * 4 + block] = jnp.concatenate(sums, axis=0)


def own(queries, aways, kv, info):
    n = len(queries)
    return pl.pallas_call(
        functools.partial(own_kernel, aways),
        out_shape=(
            jax.ShapeDtypeStruct((n * 16, DH, QBLK), BF),
            jax.ShapeDtypeStruct((n * 4, 4, QBLK), F32),
        ),
        in_specs=[SMEM] + [VMEM] * (n + 1),
        out_specs=(VMEM, VMEM),
        compiler_params=params(),
        cost_estimate=pl.CostEstimate(
            flops=n * 16 * 4 * QBLK * QBLK * DH,
            bytes_accessed=2 * n * 2**20,
            transcendentals=n * 16 * QBLK * QBLK,
        ),
        name=f"own{n}",
    )(info, kv, *queries)


def split3(x):
    high = x.astype(BF).astype(F32)
    mid = (x - high).astype(BF).astype(F32)
    return [high, mid, x - high - mid]


def merge_kernel(
    j, away, arrivals, spans, info_ref, table_ref, back_ref, own_ref, own_lse_ref, *refs
):
    half = info_ref[0] // 4
    arrived, outs = refs[: len(arrivals)], refs[len(arrivals) : -2]
    arrived_lse, new_lse = refs[-2:]
    tail_at = back_ref.shape[1] - 16
    for a, (low, count) in enumerate(arrivals):
        rows = arrived[a][count * 4].astype(F32)
        rows = rows[0:32] + rows[32:64] + rows[64:96]
        for b in range(count):
            arrived_lse[a, b] = rows[4 * b : 4 * b + 4]

    def four_tiles(b, out_ref, start):
        own_at = j * 4 + b // 2
        own_sums = own_lse_ref[own_at] + jnp.where(b % 2 == half, 0.0, NONE)
        coming = []
        for a, (low, count) in enumerate(arrivals):
            here = b - low
            inside = jnp.logical_and(here >= 0, here < count)
            here = jnp.clip(here, 0, count - 1)
            coming.append(
                (arrived[a], here, arrived_lse[a, here] + jnp.where(inside, 0.0, NONE))
            )
        sums_out = []
        for t in range(4):
            tile = b * 4 + t
            parts = [own_ref[own_at * 4 + t]]
            sums = [own_sums[t : t + 1]]
            for acc_ref, here, arrived_sums in coming:
                parts.append(acc_ref[here * 4 + t])
                sums.append(arrived_sums[t : t + 1])
            for k in range(TOPK):
                owner = table_ref[away * 128 + tile * TOPK + k]
                at = jnp.maximum(owner, 0)
                parts.append(back_ref[at, j * QBLK : (j + 1) * QBLK, :])
                tail = back_ref[at, tail_at:, :].astype(F32)
                x = tail[3 * j : 3 * j + 1] + tail[3 * j + 1 : 3 * j + 2]
                x = x + tail[3 * j + 2 : 3 * j + 3]
                sums.append(x + jnp.where(owner >= 0, 0.0, NONE))
            top = functools.reduce(jnp.maximum, sums)
            weights = [jnp.exp2(x - top) for x in sums]
            total = sum(weights)
            inverse = 1.0 / total
            value = sum(
                part.astype(F32) * (weight * inverse) for part, weight in zip(parts, weights)
            )
            if spans is None:
                rows = pl.multiple_of(tile * QBLK, QBLK)
                out_ref[pl.ds(rows, QBLK), :] = value.T.astype(BF)
            else:
                out_ref[tile - start * 4] = value.astype(BF)
                sums_out.append(top + jnp.log2(total))
        if spans is not None:
            new_lse[b] = jnp.concatenate(sums_out, axis=0)

    for out_ref, (start, stop) in zip(outs, spans or ((0, TILES // 4),)):
        pl.loop(start, stop)(functools.partial(four_tiles, out_ref=out_ref, start=start))
        if spans is not None:
            rows = [new_lse[b] for b in range(start, stop)]
            if stop - start < TILES // 4:
                rows.append(jnp.zeros((TILES - 4 * (stop - start), DH), F32))
            rows = split3(jnp.concatenate(rows, axis=0))
            rows.append(jnp.zeros((128 - 3 * TILES, DH), F32))
            out_ref[(stop - start) * 4] = jnp.concatenate(rows, axis=0).astype(BF)


def merge(j, away, info, table, back, own_part, arrivals, spans):
    places = tuple((low, (acc.shape[0] - 1) // 4) for low, acc in arrivals)
    if spans is None:
        out_shape = (jax.ShapeDtypeStruct((TILES * QBLK, DH), BF),)
    else:
        out_shape = tuple(
            jax.ShapeDtypeStruct(((stop - start) * 4 + 1, DH, QBLK), BF) for start, stop in spans
        )
    return pl.pallas_call(
        functools.partial(merge_kernel, j, away, places, spans),
        out_shape=out_shape,
        in_specs=[SMEM, SMEM] + [VMEM] * (3 + len(arrivals)),
        out_specs=(VMEM,) * len(out_shape),
        scratch_shapes=[
            pltpu.VMEM((max(1, len(arrivals)), TILES // 4, 4, QBLK), F32),
            pltpu.VMEM((TILES // 4, 4, QBLK), F32),
        ],
        compiler_params=params(),
        cost_estimate=pl.CostEstimate(
            flops=TILES * 12 * QBLK * DH, bytes_accessed=4 * 2**20, transcendentals=0
        ),
        name=f"merge{j}",
    )(info, table, back, *own_part, *[acc for _, acc in arrivals])


def ring(x, step, axis="z", size=NZ):
    return lax.ppermute(x, axis, [(i, (i + step) % size) for i in range(size)])


def after(x, *others):
    return lax.optimization_barrier((x,) + others)[0]


CHUNKS = ((0,), (1, 7), (2, 6), (3, 5), (4,))


def shards(queries, win_key, win_value, past_key, past_value, chosen):
    x, z = lax.axis_index("x"), lax.axis_index("z")

    with jax.named_scope("prepare"):
        tiles = queries.reshape(TILES, QBLK, DH).swapaxes(1, 2)
        mine = jnp.pad(chosen.reshape(1, REQ), ((0, 0), (0, 128 - REQ)), constant_values=-4)

    with jax.named_scope("column"):
        away = (z + jnp.arange(NZ, dtype=jnp.int32)) % NZ
        column = lax.all_to_all(jnp.broadcast_to(mine, (NZ, 128)), "z", 0, 0, tiled=True)
    right = left = tiles
    sources = [(tiles,)]
    for step in range(1, 4):
        with jax.named_scope(f"ring{step}"):
            right, left = ring(right, 1), ring(left, -1)
        sources.append((left, right))
    with jax.named_scope("ring4"):
        sources.append((jnp.concatenate([ring(right[:16], 1), ring(left[16:], -1)], axis=0),))

    def coded(lists):
        plane_ids = jnp.arange(PLANE, dtype=jnp.int32)
        owner_ids = (plane_ids // 4) * 32 + (plane_ids % 4) * 8 + z
        entry = jnp.arange(128, dtype=jnp.int32) // TOPK * 4 + lists % 4 + 1
        found = jnp.where((lists // 4)[None] == owner_ids[:, None, None], entry[None], 0)
        return jnp.sum(found, axis=2)

    def tiles_in(code):
        return (jnp.maximum(code - 1, 0) // 4).reshape(-1)

    with jax.named_scope("lists"):
        tile_of_mine = tiles_in(coded(mine))
        column = jnp.take(column, away, axis=0)
        owner = column // 4
        code = coded(column)
        group = 2 * x + away // 4
        meta = jnp.where(code > 0, (code - 1) % 4 * 8 + group[None], -1)
        meta = jnp.pad(meta, ((0, 0), (0, 128 - NZ)))
        tile_of = tiles_in(code)
        place = (owner // 32) * 4 + owner % 32 // 8
        table = jnp.where(jnp.logical_and(owner % 8 == z, owner >= 0), place, -1).reshape(-1)
        info = jnp.where(jnp.arange(128, dtype=jnp.int32) == 0, z, x)
        meta, table, tile_of, info = lax.optimization_barrier((meta, table, tile_of, info))

    with jax.named_scope("kv"):
        own_k = win_key.reshape(QBLK, 4, 2, DH).transpose(1, 2, 0, 3)
        own_v = win_value.reshape(QBLK, 4, 2, DH).transpose(1, 2, 3, 0)
        pieces = jnp.concatenate([own_k, own_v], axis=1)
        kv = [lax.dynamic_index_in_dim(pieces, x, axis=0, keepdims=False)]
        for d in range(1, 4):
            piece = lax.dynamic_index_in_dim(pieces, (x + d) % 4, axis=0, keepdims=False)
            kv.append(ring(piece, d, "x", 4))
        kv = jnp.stack(kv)
        past_value_t = past_value.T

    previous = []

    def exchange(send, *others):
        send = after(send, *previous, *others)
        got = lax.all_to_all(send, ("y", "c", "x"), 0, 0, tiled=True)
        previous[:] = [got]
        return got

    def forward(chunks, *others):
        refs = [t for c in chunks for t in sources[c]]
        aways = [d for c in chunks for d in CHUNKS[c]]
        return exchange(pack(refs, aways, tile_of), *others)

    def partial(c, got, first=0):
        with jax.named_scope(f"far{c}"):
            return far(got, first, CHUNKS[c], meta, past_key, past_value_t)

    def own_part(c):
        with jax.named_scope(f"own{c}"):
            return tuple(own(sources[c], CHUNKS[c], kv, info))

    def merged(c, back, arrivals):
        out = {}
        with jax.named_scope(f"merge{c}"):
            for low in (0, 4):
                for j, away_by in enumerate(CHUNKS[c]):
                    coming = arrivals.get((j, low), [])
                    coming = [(low, acc) for acc in coming]
                    span = ((low, low + 4),)
                    (out[j, low],) = merge(
                        j, away_by, info, table, back, owns[c], coming, span
                    )
        return out

    def onward(c, parts):
        with jax.named_scope(f"return{c}"):
            return {(j, low): [ring(acc, 1 - 2 * j)] for (j, low), acc in parts.items()}

    def arrived(arrivals):
        return [acc for (acc,) in arrivals.values()]

    with jax.named_scope("forward"):
        got0 = exchange(pack(sources[0], (0,), tile_of_mine), column, *sources[1])
        own0, own1 = own_part(0), own_part(1)
        meta = exchange(meta, past_value_t, *own0, *own1)[:, :NZ].reshape(-1)
        got12 = forward((1, 2))
        part0, own2 = partial(0, got0), own_part(2)
        got34 = forward((3, 4), part0, *own2)
        part2, own3, own4 = partial(2, got12, 2), own_part(3), own_part(4)
        part4 = partial(4, after(got34, part2, *own3, *own4), 2)
        part3, part1 = partial(3, got34), partial(1, got12)
    owns = [own0, own1, own2, own3, own4]
    with jax.named_scope("back"):
        back4 = exchange(part4)
        back3 = exchange(part3)
        parts = merged(4, back4, {})
        arrivals = onward(4, {(0, 0): parts[0, 0], (1, 4): parts[0, 4]})
        back2 = exchange(part2, part1, *arrived(arrivals))
        arrivals = onward(3, merged(3, back3, arrivals))
        back1 = exchange(part1, *arrived(arrivals))
        arrivals = onward(2, merged(2, back2, arrivals))
        back0 = exchange(part0, *arrived(arrivals))
        arrivals = onward(1, merged(1, back1, arrivals))
        arrivals = [(low, acc) for (_, low), (acc,) in arrivals.items()]
        return merge(0, 0, info, table, back0, own0, arrivals, None)[0]


def solution(mesh):
    inner = Mesh(mesh.devices.reshape(4, 2, 4, 8), ("y", "c", "x", "z"))
    rows, heads = ("y", "c"), ("x", "z")
    return jax.shard_map(
        shards,
        mesh=inner,
        in_specs=(
            P(rows, heads),
            P(rows + heads, None),
            P(rows + heads, None),
            P(rows + heads, None),
            P(rows + heads, None),
            P(rows, heads, None),
        ),
        out_specs=P(rows, heads),
        check_vma=False,
    )
```

```python
import functools
import math

import jax
import jax.numpy as jnp
from jax import lax
from jax.experimental import pallas as pl
from jax.experimental.pallas import tpu as pltpu
from jax.sharding import Mesh, PartitionSpec as P

DH = 128
BLK = 512
QBLK = 128
TOPK = 3
TILES = 32
PLANE = 32
NZ = 8
REQ = 96
UNROLL = 4
EXP_SCALE = math.log2(math.e) / math.sqrt(DH)
NONE = -1e30
BF = jnp.bfloat16
F32 = jnp.float32

VMEM = pl.BlockSpec(memory_space=pltpu.VMEM)
SMEM = pl.BlockSpec(memory_space=pltpu.SMEM)
ANY = pl.BlockSpec(memory_space=pl.ANY)


def params():
    return pltpu.CompilerParams(vmem_limit_bytes=48 * 1024 * 1024)


def mxu(a, b):
    return jnp.dot(a, b, preferred_element_type=F32)


def pack_kernel(aways, stride, idx_ref, *refs):
    n = len(aways)
    sources, out_ref, sem = refs[:n], refs[n], refs[n + 1]

    @pl.loop(0, PLANE)
    def _(owner):
        for j in range(n):
            pltpu.make_async_copy(
                sources[j].at[idx_ref[owner * stride + aways[j]]],
                out_ref.at[owner, pl.ds(j * QBLK, QBLK), :],
                sem,
            ).start()

    pltpu.make_async_copy(out_ref, out_ref, sem).wait()


def pack(sources, aways, idx):
    stride = idx.shape[0] // PLANE
    n = len(sources)
    return pl.pallas_call(
        functools.partial(pack_kernel, aways, stride),
        out_shape=jax.ShapeDtypeStruct((PLANE, n * QBLK, DH), BF),
        in_specs=[SMEM] + [VMEM] * n,
        out_specs=ANY,
        scratch_shapes=[pltpu.SemaphoreType.DMA],
        compiler_params=params(),
        cost_estimate=pl.CostEstimate(
            flops=0, bytes_accessed=2 * n * PLANE * QBLK * DH * 2, transcendentals=0
        ),
        name=f"pack{n}",
    )(idx, *sources)


def far_kernel(
    aways, first, meta_ref, got_ref, k_ref, vt_ref, out_ref, q_ref, lse_ref, list_ref, sem
):
    n = len(aways)
    slots = PLANE * n

    def meta_of(slot):
        if n == 1:
            return meta_ref[slot * NZ + aways[0]]
        return meta_ref[slot // 2 * NZ + jnp.where(slot % 2 == 0, aways[0], aways[1])]

    copy = pltpu.make_async_copy(
        got_ref.at[:, first * QBLK : (first + n) * QBLK, :], q_ref, sem
    )
    copy.start()
    out_ref[...] = jnp.zeros_like(out_ref)
    lse_ref[...] = jnp.zeros_like(lse_ref)

    def listed(i, count):
        list_ref[count] = i
        return count + (meta_of(i) >= 0).astype(jnp.int32)

    count = lax.fori_loop(0, slots, listed, jnp.int32(0))
    last = list_ref[jnp.maximum(count - 1, 0)]
    for u in range(UNROLL):
        list_ref[count + u] = last
    copy.wait()

    @pl.loop(0, (count + UNROLL - 1) // UNROLL)
    def _(turn):
        ids = [list_ref[turn * UNROLL + u] for u in range(UNROLL)]
        scores, values = [], []
        for slot in ids:
            meta = meta_of(slot)
            keys = pl.multiple_of((meta // 8) * BLK, BLK)
            cols = pl.multiple_of((meta % 8) * DH, DH)
            q = q_ref[slot // n, pl.ds(pl.multiple_of(slot % n * QBLK, QBLK), QBLK), :]
            scores.append(mxu(k_ref[pl.ds(keys, BLK), pl.ds(cols, DH)], q))
            values.append(vt_ref[pl.ds(cols, DH), pl.ds(keys, BLK)])
        tops = [jnp.max(s, axis=0, keepdims=True) for s in scores]
        terms = [jnp.exp2((s - m) * EXP_SCALE) for s, m in zip(scores, tops)]
        totals = [jnp.sum(t, axis=0, keepdims=True) for t in terms]
        outs = [mxu(v, t.astype(BF)) for v, t in zip(values, terms)]
        for slot, o, m, l in zip(ids, outs, tops, totals):
            out_ref[slot // n, pl.ds(pl.multiple_of(slot % n * QBLK, QBLK), QBLK), :] = (
                o * (1.0 / l)
            ).astype(BF)
            lse_ref[slot] = m * EXP_SCALE + jnp.log2(l)

    @pl.loop(0, PLANE)
    def _(source):
        rows = []
        for j in range(n):
            rows += split3(lse_ref[source * n + j])
        rows.append(jnp.zeros((16 - len(rows), DH), F32))
        out_ref[source, n * QBLK :, :] = jnp.concatenate(rows, axis=0).astype(BF)


def far(tiles, first, aways, meta, past_key, past_value_t):
    n = len(aways)
    slots = PLANE * n
    return pl.pallas_call(
        functools.partial(far_kernel, aways, first),
        out_shape=jax.ShapeDtypeStruct((PLANE, n * QBLK + 16, DH), BF),
        in_specs=[SMEM, ANY, VMEM, VMEM],
        out_specs=VMEM,
        scratch_shapes=[
            pltpu.VMEM((PLANE, n * QBLK, DH), BF),
            pltpu.VMEM((slots, 1, DH), F32),
            pltpu.SMEM((slots + UNROLL,), jnp.int32),
            pltpu.SemaphoreType.DMA,
        ],
        compiler_params=params(),
        cost_estimate=pl.CostEstimate(
            flops=slots * 4 * QBLK * BLK * DH,
            bytes_accessed=12 * 2**20,
            transcendentals=slots * QBLK * BLK,
        ),
        name=f"far{n}",
    )(meta, tiles, past_key, past_value_t)


def own_kernel(aways, info_ref, kv_ref, *refs):
    n = len(aways)
    queries, out_ref, lse_ref = refs[:n], refs[n], refs[n + 1]
    z, column = info_ref[0], info_ref[1]
    half, part = z // 4, z % 4
    key_at = lax.broadcasted_iota(jnp.int32, (QBLK, QBLK), 0)
    row_at = lax.broadcasted_iota(jnp.int32, (QBLK, QBLK), 1)
    for j in range(n):
        group = (z + aways[j]) % NZ // 4

        @pl.loop(0, 4)
        def _(b):
            keys = kv_ref[b, group]
            values = kv_ref[b, 2 + group]
            block = (column - b + 4) % 4
            first = (block * 2 + half) * 4
            scores = [mxu(keys, queries[j][first + t]) for t in range(4)]
            scores = [
                jnp.where(key_at <= row_at + (t - part) * QBLK, s, NONE)
                for t, s in enumerate(scores)
            ]
            tops = [jnp.max(s, axis=0, keepdims=True) for s in scores]
            terms = [jnp.exp2((s - m) * EXP_SCALE) for s, m in zip(scores, tops)]
            totals = [jnp.sum(t, axis=0, keepdims=True) for t in terms]
            outs = [mxu(values, t.astype(BF)) for t in terms]
            sums = []
            for t in range(4):
                out_ref[j * 16 + block * 4 + t] = (outs[t] * (1.0 / totals[t])).astype(BF)
                x = tops[t] * EXP_SCALE + jnp.log2(totals[t])
                sums.append(x + jnp.where(part > t, NONE, 0.0))
            lse_ref[j * 4 + block] = jnp.concatenate(sums, axis=0)


def own(queries, aways, kv, info):
    n = len(queries)
    return pl.pallas_call(
        functools.partial(own_kernel, aways),
        out_shape=(
            jax.ShapeDtypeStruct((n * 16, DH, QBLK), BF),
            jax.ShapeDtypeStruct((n * 4, 4, QBLK), F32),
        ),
        in_specs=[SMEM] + [VMEM] * (n + 1),
        out_specs=(VMEM, VMEM),
        compiler_params=params(),
        cost_estimate=pl.CostEstimate(
            flops=n * 16 * 4 * QBLK * QBLK * DH,
            bytes_accessed=2 * n * 2**20,
            transcendentals=n * 16 * QBLK * QBLK,
        ),
        name=f"own{n}",
    )(info, kv, *queries)


def split3(x):
    high = x.astype(BF).astype(F32)
    mid = (x - high).astype(BF).astype(F32)
    return [high, mid, x - high - mid]


def merge_kernel(
    j, away, arrivals, spans, info_ref, table_ref, back_ref, own_ref, own_lse_ref, *refs
):
    half = info_ref[0] // 4
    arrived, outs = refs[: len(arrivals)], refs[len(arrivals) : -2]
    arrived_lse, new_lse = refs[-2:]
    tail_at = back_ref.shape[1] - 16
    for a, (low, count) in enumerate(arrivals):
        rows = arrived[a][count * 4].astype(F32)
        rows = rows[0:32] + rows[32:64] + rows[64:96]
        for b in range(count):
            arrived_lse[a, b] = rows[4 * b : 4 * b + 4]

    def four_tiles(b, out_ref, start):
        own_at = j * 4 + b // 2
        own_sums = own_lse_ref[own_at] + jnp.where(b % 2 == half, 0.0, NONE)
        coming = []
        for a, (low, count) in enumerate(arrivals):
            here = b - low
            inside = jnp.logical_and(here >= 0, here < count)
            here = jnp.clip(here, 0, count - 1)
            coming.append(
                (arrived[a], here, arrived_lse[a, here] + jnp.where(inside, 0.0, NONE))
            )
        sums_out = []
        for t in range(4):
            tile = b * 4 + t
            parts = [own_ref[own_at * 4 + t]]
            sums = [own_sums[t : t + 1]]
            for acc_ref, here, arrived_sums in coming:
                parts.append(acc_ref[here * 4 + t])
                sums.append(arrived_sums[t : t + 1])
            for k in range(TOPK):
                owner = table_ref[away * 128 + tile * TOPK + k]
                at = jnp.maximum(owner, 0)
                parts.append(back_ref[at, j * QBLK : (j + 1) * QBLK, :])
                tail = back_ref[at, tail_at:, :].astype(F32)
                x = tail[3 * j : 3 * j + 1] + tail[3 * j + 1 : 3 * j + 2]
                x = x + tail[3 * j + 2 : 3 * j + 3]
                sums.append(x + jnp.where(owner >= 0, 0.0, NONE))
            top = functools.reduce(jnp.maximum, sums)
            weights = [jnp.exp2(x - top) for x in sums]
            total = sum(weights)
            inverse = 1.0 / total
            value = sum(
                part.astype(F32) * (weight * inverse) for part, weight in zip(parts, weights)
            )
            if spans is None:
                rows = pl.multiple_of(tile * QBLK, QBLK)
                out_ref[pl.ds(rows, QBLK), :] = value.T.astype(BF)
            else:
                out_ref[tile - start * 4] = value.astype(BF)
                sums_out.append(top + jnp.log2(total))
        if spans is not None:
            new_lse[b] = jnp.concatenate(sums_out, axis=0)

    for out_ref, (start, stop) in zip(outs, spans or ((0, TILES // 4),)):
        pl.loop(start, stop)(functools.partial(four_tiles, out_ref=out_ref, start=start))
        if spans is not None:
            rows = [new_lse[b] for b in range(start, stop)]
            if stop - start < TILES // 4:
                rows.append(jnp.zeros((TILES - 4 * (stop - start), DH), F32))
            rows = split3(jnp.concatenate(rows, axis=0))
            rows.append(jnp.zeros((128 - 3 * TILES, DH), F32))
            out_ref[(stop - start) * 4] = jnp.concatenate(rows, axis=0).astype(BF)


def merge(j, away, info, table, back, own_part, arrivals, spans):
    places = tuple((low, (acc.shape[0] - 1) // 4) for low, acc in arrivals)
    if spans is None:
        out_shape = (jax.ShapeDtypeStruct((TILES * QBLK, DH), BF),)
    else:
        out_shape = tuple(
            jax.ShapeDtypeStruct(((stop - start) * 4 + 1, DH, QBLK), BF) for start, stop in spans
        )
    return pl.pallas_call(
        functools.partial(merge_kernel, j, away, places, spans),
        out_shape=out_shape,
        in_specs=[SMEM, SMEM] + [VMEM] * (3 + len(arrivals)),
        out_specs=(VMEM,) * len(out_shape),
        scratch_shapes=[
            pltpu.VMEM((max(1, len(arrivals)), TILES // 4, 4, QBLK), F32),
            pltpu.VMEM((TILES // 4, 4, QBLK), F32),
        ],
        compiler_params=params(),
        cost_estimate=pl.CostEstimate(
            flops=TILES * 12 * QBLK * DH, bytes_accessed=4 * 2**20, transcendentals=0
        ),
        name=f"merge{j}",
    )(info, table, back, *own_part, *[acc for _, acc in arrivals])


def ring(x, step, axis="z", size=NZ):
    return lax.ppermute(x, axis, [(i, (i + step) % size) for i in range(size)])


def after(x, *others):
    return lax.optimization_barrier((x,) + others)[0]


CHUNKS = ((0,), (1, 7), (2, 6), (3, 5), (4,))


def shards(queries, win_key, win_value, past_key, past_value, chosen):
    x, z = lax.axis_index("x"), lax.axis_index("z")

    with jax.named_scope("prepare"):
        tiles = queries.reshape(TILES, QBLK, DH).swapaxes(1, 2)
        mine = jnp.pad(chosen.reshape(1, REQ), ((0, 0), (0, 128 - REQ)), constant_values=-4)

    with jax.named_scope("column"):
        away = (z + jnp.arange(NZ, dtype=jnp.int32)) % NZ
        column = lax.all_to_all(jnp.broadcast_to(mine, (NZ, 128)), "z", 0, 0, tiled=True)
    right = left = tiles
    sources = [(tiles,)]
    for step in range(1, 4):
        with jax.named_scope(f"ring{step}"):
            right, left = ring(right, 1), ring(left, -1)
        sources.append((left, right))
    with jax.named_scope("ring4"):
        sources.append((jnp.concatenate([ring(right[:16], 1), ring(left[16:], -1)], axis=0),))

    def coded(lists):
        plane_ids = jnp.arange(PLANE, dtype=jnp.int32)
        owner_ids = (plane_ids // 4) * 32 + (plane_ids % 4) * 8 + z
        entry = jnp.arange(128, dtype=jnp.int32) // TOPK * 4 + lists % 4 + 1
        found = jnp.where((lists // 4)[None] == owner_ids[:, None, None], entry[None], 0)
        return jnp.sum(found, axis=2)

    def tiles_in(code):
        return (jnp.maximum(code - 1, 0) // 4).reshape(-1)

    with jax.named_scope("lists"):
        tile_of_mine = tiles_in(coded(mine))
        column = jnp.take(column, away, axis=0)
        owner = column // 4
        code = coded(column)
        group = 2 * x + away // 4
        meta = jnp.where(code > 0, (code - 1) % 4 * 8 + group[None], -1)
        meta = jnp.pad(meta, ((0, 0), (0, 128 - NZ)))
        tile_of = tiles_in(code)
        place = (owner // 32) * 4 + owner % 32 // 8
        table = jnp.where(jnp.logical_and(owner % 8 == z, owner >= 0), place, -1).reshape(-1)
        info = jnp.where(jnp.arange(128, dtype=jnp.int32) == 0, z, x)
        meta, table, tile_of, info = lax.optimization_barrier((meta, table, tile_of, info))

    with jax.named_scope("kv"):
        own_k = win_key.reshape(QBLK, 4, 2, DH).transpose(1, 2, 0, 3)
        own_v = win_value.reshape(QBLK, 4, 2, DH).transpose(1, 2, 3, 0)
        pieces = jnp.concatenate([own_k, own_v], axis=1)
        kv = [lax.dynamic_index_in_dim(pieces, x, axis=0, keepdims=False)]
        for d in range(1, 4):
            piece = lax.dynamic_index_in_dim(pieces, (x + d) % 4, axis=0, keepdims=False)
            kv.append(ring(piece, d, "x", 4))
        kv = jnp.stack(kv)
        past_value_t = past_value.T

    previous = []

    def exchange(send, *others):
        send = after(send, *previous, *others)
        got = lax.all_to_all(send, ("y", "c", "x"), 0, 0, tiled=True)
        previous[:] = [got]
        return got

    def forward(chunks, *others):
        refs = [t for c in chunks for t in sources[c]]
        aways = [d for c in chunks for d in CHUNKS[c]]
        return exchange(pack(refs, aways, tile_of), *others)

    def partial(c, got, first=0):
        with jax.named_scope(f"far{c}"):
            return far(got, first, CHUNKS[c], meta, past_key, past_value_t)

    def own_part(c):
        with jax.named_scope(f"own{c}"):
            return tuple(own(sources[c], CHUNKS[c], kv, info))

    def merged(c, back, arrivals, spans=((0, 8),)):
        out = []
        with jax.named_scope(f"merge{c}"):
            for span in spans:
                for j, away_by in enumerate(CHUNKS[c]):
                    coming = [
                        (low, acc)
                        for (at, low, high), acc in arrivals
                        if at == j and low < span[1] and high > span[0]
                    ]
                    (acc,) = merge(j, away_by, info, table, back, owns[c], coming, (span,))
                    out.append(((j,) + span, acc))
        return out

    def onward(c, parts):
        with jax.named_scope(f"return{c}"):
            return [(key, ring(acc, 1 - 2 * key[0])) for key, acc in parts]

    def arrays(arrivals):
        return [acc for _, acc in arrivals]

    with jax.named_scope("forward"):
        got0 = exchange(pack(sources[0], (0,), tile_of_mine), column, *sources[1])
        own0, own1 = own_part(0), own_part(1)
        meta = exchange(meta, past_value_t, *own0, *own1)[:, :NZ].reshape(-1)
        got12 = forward((1, 2))
        part0, own2 = partial(0, got0), own_part(2)
        got34 = forward((3, 4), part0, *own2)
        part2, own3, own4 = partial(2, got12, 2), own_part(3), own_part(4)
        part4 = partial(4, after(got34, part2, *own3, *own4), 2)
        part3, part1 = partial(3, got34), partial(1, got12)
    owns = [own0, own1, own2, own3, own4]
    with jax.named_scope("back"):
        back4 = exchange(part4)
        back3 = exchange(part3)
        (low, high) = merged(4, back4, [], ((0, 4), (4, 8)))
        arrivals = onward(4, [((0, 0, 4), low[1]), ((1, 4, 8), high[1])])
        back2 = exchange(part2, part1, *arrays(arrivals))
        arrivals = onward(3, merged(3, back3, arrivals))
        back1 = exchange(part1, *arrays(arrivals))
        arrivals = onward(2, merged(2, back2, arrivals))
        back0 = exchange(part0)
        arrivals = onward(1, merged(1, back1, arrivals))
        arrivals = [(low, acc) for (_, low, _), acc in arrivals]
        return merge(0, 0, info, table, back0, own0, arrivals, None)[0]


def solution(mesh):
    inner = Mesh(mesh.devices.reshape(4, 2, 4, 8), ("y", "c", "x", "z"))
    rows, heads = ("y", "c"), ("x", "z")
    return jax.shard_map(
        shards,
        mesh=inner,
        in_specs=(
            P(rows, heads),
            P(rows + heads, None),
            P(rows + heads, None),
            P(rows + heads, None),
            P(rows + heads, None),
            P(rows, heads, None),
        ),
        out_specs=P(rows, heads),
        check_vma=False,
    )
```

```python
import functools
import math

import jax
import jax.numpy as jnp
from jax import lax
from jax.experimental import pallas as pl
from jax.experimental.pallas import tpu as pltpu
from jax.sharding import Mesh, PartitionSpec as P

DH = 128
BLK = 512
QBLK = 128
TOPK = 3
TILES = 32
PLANE = 32
NZ = 8
REQ = 96
UNROLL = 4
EXP_SCALE = math.log2(math.e) / math.sqrt(DH)
NONE = -1e30
BF = jnp.bfloat16
F32 = jnp.float32

VMEM = pl.BlockSpec(memory_space=pltpu.VMEM)
SMEM = pl.BlockSpec(memory_space=pltpu.SMEM)
ANY = pl.BlockSpec(memory_space=pl.ANY)


def params():
    return pltpu.CompilerParams(vmem_limit_bytes=48 * 1024 * 1024)


def mxu(a, b):
    return jnp.dot(a, b, preferred_element_type=F32)


def pack_kernel(aways, stride, idx_ref, *refs):
    n = len(aways)
    sources, out_ref, sem = refs[:n], refs[n], refs[n + 1]

    @pl.loop(0, PLANE)
    def _(owner):
        for j in range(n):
            pltpu.make_async_copy(
                sources[j].at[idx_ref[owner * stride + aways[j]]],
                out_ref.at[owner, pl.ds(j * QBLK, QBLK), :],
                sem,
            ).start()

    pltpu.make_async_copy(out_ref, out_ref, sem).wait()


def pack(sources, aways, idx):
    stride = idx.shape[0] // PLANE
    n = len(sources)
    return pl.pallas_call(
        functools.partial(pack_kernel, aways, stride),
        out_shape=jax.ShapeDtypeStruct((PLANE, n * QBLK, DH), BF),
        in_specs=[SMEM] + [VMEM] * n,
        out_specs=ANY,
        scratch_shapes=[pltpu.SemaphoreType.DMA],
        compiler_params=params(),
        cost_estimate=pl.CostEstimate(
            flops=0, bytes_accessed=2 * n * PLANE * QBLK * DH * 2, transcendentals=0
        ),
        name=f"pack{n}",
    )(idx, *sources)


def far_kernel(
    aways, first, meta_ref, got_ref, k_ref, vt_ref, out_ref, q_ref, lse_ref, list_ref, sem
):
    n = len(aways)
    slots = PLANE * n

    def meta_of(slot):
        if n == 1:
            return meta_ref[slot * NZ + aways[0]]
        return meta_ref[slot // 2 * NZ + jnp.where(slot % 2 == 0, aways[0], aways[1])]

    copy = pltpu.make_async_copy(
        got_ref.at[:, first * QBLK : (first + n) * QBLK, :], q_ref, sem
    )
    copy.start()
    out_ref[...] = jnp.zeros_like(out_ref)
    lse_ref[...] = jnp.zeros_like(lse_ref)

    def listed(i, count):
        list_ref[count] = i
        return count + (meta_of(i) >= 0).astype(jnp.int32)

    count = lax.fori_loop(0, slots, listed, jnp.int32(0))
    last = list_ref[jnp.maximum(count - 1, 0)]
    for u in range(UNROLL):
        list_ref[count + u] = last
    copy.wait()

    @pl.loop(0, (count + UNROLL - 1) // UNROLL)
    def _(turn):
        ids = [list_ref[turn * UNROLL + u] for u in range(UNROLL)]
        scores, values = [], []
        for slot in ids:
            meta = meta_of(slot)
            keys = pl.multiple_of((meta // 8) * BLK, BLK)
            cols = pl.multiple_of((meta % 8) * DH, DH)
            q = q_ref[slot // n, pl.ds(pl.multiple_of(slot % n * QBLK, QBLK), QBLK), :]
            scores.append(mxu(k_ref[pl.ds(keys, BLK), pl.ds(cols, DH)], q))
            values.append(vt_ref[pl.ds(cols, DH), pl.ds(keys, BLK)])
        tops = [jnp.max(s, axis=0, keepdims=True) for s in scores]
        terms = [jnp.exp2((s - m) * EXP_SCALE) for s, m in zip(scores, tops)]
        totals = [jnp.sum(t, axis=0, keepdims=True) for t in terms]
        outs = [mxu(v, t.astype(BF)) for v, t in zip(values, terms)]
        for slot, o, m, l in zip(ids, outs, tops, totals):
            out_ref[slot // n, pl.ds(pl.multiple_of(slot % n * QBLK, QBLK), QBLK), :] = (
                o * (1.0 / l)
            ).astype(BF)
            lse_ref[slot] = m * EXP_SCALE + jnp.log2(l)

    @pl.loop(0, PLANE)
    def _(source):
        rows = []
        for j in range(n):
            rows += split3(lse_ref[source * n + j])
        rows.append(jnp.zeros((16 - len(rows), DH), F32))
        out_ref[source, n * QBLK :, :] = jnp.concatenate(rows, axis=0).astype(BF)


def far(tiles, first, aways, meta, past_key, past_value_t):
    n = len(aways)
    slots = PLANE * n
    return pl.pallas_call(
        functools.partial(far_kernel, aways, first),
        out_shape=jax.ShapeDtypeStruct((PLANE, n * QBLK + 16, DH), BF),
        in_specs=[SMEM, ANY, VMEM, VMEM],
        out_specs=VMEM,
        scratch_shapes=[
            pltpu.VMEM((PLANE, n * QBLK, DH), BF),
            pltpu.VMEM((slots, 1, DH), F32),
            pltpu.SMEM((slots + UNROLL,), jnp.int32),
            pltpu.SemaphoreType.DMA,
        ],
        compiler_params=params(),
        cost_estimate=pl.CostEstimate(
            flops=slots * 4 * QBLK * BLK * DH,
            bytes_accessed=12 * 2**20,
            transcendentals=slots * QBLK * BLK,
        ),
        name=f"far{n}",
    )(meta, tiles, past_key, past_value_t)


def own_kernel(aways, info_ref, kv_ref, *refs):
    n = len(aways)
    queries, out_ref, lse_ref = refs[:n], refs[n], refs[n + 1]
    z, column = info_ref[0], info_ref[1]
    half, part = z // 4, z % 4
    key_at = lax.broadcasted_iota(jnp.int32, (QBLK, QBLK), 0)
    row_at = lax.broadcasted_iota(jnp.int32, (QBLK, QBLK), 1)
    for j in range(n):
        group = (z + aways[j]) % NZ // 4

        @pl.loop(0, 4)
        def _(b):
            keys = kv_ref[b, group]
            values = kv_ref[b, 2 + group]
            block = (column - b + 4) % 4
            first = (block * 2 + half) * 4
            scores = [mxu(keys, queries[j][first + t]) for t in range(4)]
            scores = [
                jnp.where(key_at <= row_at + (t - part) * QBLK, s, NONE)
                for t, s in enumerate(scores)
            ]
            tops = [jnp.max(s, axis=0, keepdims=True) for s in scores]
            terms = [jnp.exp2((s - m) * EXP_SCALE) for s, m in zip(scores, tops)]
            totals = [jnp.sum(t, axis=0, keepdims=True) for t in terms]
            outs = [mxu(values, t.astype(BF)) for t in terms]
            sums = []
            for t in range(4):
                out_ref[j * 16 + block * 4 + t] = (outs[t] * (1.0 / totals[t])).astype(BF)
                x = tops[t] * EXP_SCALE + jnp.log2(totals[t])
                sums.append(x + jnp.where(part > t, NONE, 0.0))
            lse_ref[j * 4 + block] = jnp.concatenate(sums, axis=0)


def own(queries, aways, kv, info):
    n = len(queries)
    return pl.pallas_call(
        functools.partial(own_kernel, aways),
        out_shape=(
            jax.ShapeDtypeStruct((n * 16, DH, QBLK), BF),
            jax.ShapeDtypeStruct((n * 4, 4, QBLK), F32),
        ),
        in_specs=[SMEM] + [VMEM] * (n + 1),
        out_specs=(VMEM, VMEM),
        compiler_params=params(),
        cost_estimate=pl.CostEstimate(
            flops=n * 16 * 4 * QBLK * QBLK * DH,
            bytes_accessed=2 * n * 2**20,
            transcendentals=n * 16 * QBLK * QBLK,
        ),
        name=f"own{n}",
    )(info, kv, *queries)


def split3(x):
    high = x.astype(BF).astype(F32)
    mid = (x - high).astype(BF).astype(F32)
    return [high, mid, x - high - mid]


def merge_kernel(
    j, away, arrivals, spans, marks, info_ref, table_ref, back_ref, own_ref, own_lse_ref, *refs
):
    half = info_ref[0] // 4
    arrived, outs = refs[: len(arrivals)], refs[len(arrivals) + marks : -2]
    arrived_lse, new_lse = refs[-2:]
    tail_at = back_ref.shape[1] - 16
    for a, (low, count) in enumerate(arrivals):
        rows = arrived[a][count * 4].astype(F32)
        rows = rows[0:32] + rows[32:64] + rows[64:96]
        for b in range(count):
            arrived_lse[a, b] = rows[4 * b : 4 * b + 4]

    def four_tiles(b, out_ref, start):
        own_at = j * 4 + b // 2
        own_sums = own_lse_ref[own_at] + jnp.where(b % 2 == half, 0.0, NONE)
        coming = []
        for a, (low, count) in enumerate(arrivals):
            here = b - low
            inside = jnp.logical_and(here >= 0, here < count)
            here = jnp.clip(here, 0, count - 1)
            coming.append(
                (arrived[a], here, arrived_lse[a, here] + jnp.where(inside, 0.0, NONE))
            )
        sums_out = []
        for t in range(4):
            tile = b * 4 + t
            parts = [own_ref[own_at * 4 + t]]
            sums = [own_sums[t : t + 1]]
            for acc_ref, here, arrived_sums in coming:
                parts.append(acc_ref[here * 4 + t])
                sums.append(arrived_sums[t : t + 1])
            for k in range(TOPK):
                owner = table_ref[away * 128 + tile * TOPK + k]
                at = jnp.maximum(owner, 0)
                parts.append(back_ref[at, j * QBLK : (j + 1) * QBLK, :])
                tail = back_ref[at, tail_at:, :].astype(F32)
                x = tail[3 * j : 3 * j + 1] + tail[3 * j + 1 : 3 * j + 2]
                x = x + tail[3 * j + 2 : 3 * j + 3]
                sums.append(x + jnp.where(owner >= 0, 0.0, NONE))
            top = functools.reduce(jnp.maximum, sums)
            weights = [jnp.exp2(x - top) for x in sums]
            total = sum(weights)
            inverse = 1.0 / total
            value = sum(
                part.astype(F32) * (weight * inverse) for part, weight in zip(parts, weights)
            )
            if spans is None:
                rows = pl.multiple_of(tile * QBLK, QBLK)
                out_ref[pl.ds(rows, QBLK), :] = value.T.astype(BF)
            else:
                out_ref[tile - start * 4] = value.astype(BF)
                sums_out.append(top + jnp.log2(total))
        if spans is not None:
            new_lse[b] = jnp.concatenate(sums_out, axis=0)

    for out_ref, (start, stop) in zip(outs, spans or ((0, TILES // 4),)):
        pl.loop(start, stop)(functools.partial(four_tiles, out_ref=out_ref, start=start))
        if spans is not None:
            rows = [new_lse[b] for b in range(start, stop)]
            if stop - start < TILES // 4:
                rows.append(jnp.zeros((TILES - 4 * (stop - start), DH), F32))
            rows = split3(jnp.concatenate(rows, axis=0))
            rows.append(jnp.zeros((128 - 3 * TILES, DH), F32))
            out_ref[(stop - start) * 4] = jnp.concatenate(rows, axis=0).astype(BF)


def merge(j, away, info, table, back, own_part, arrivals, spans, mark=()):
    places = tuple((low, (acc.shape[0] - 1) // 4) for low, acc in arrivals)
    if spans is None:
        out_shape = (jax.ShapeDtypeStruct((TILES * QBLK, DH), BF),)
    else:
        out_shape = tuple(
            jax.ShapeDtypeStruct(((stop - start) * 4 + 1, DH, QBLK), BF) for start, stop in spans
        )
    return pl.pallas_call(
        functools.partial(merge_kernel, j, away, places, spans, len(mark)),
        out_shape=out_shape,
        in_specs=[SMEM, SMEM] + [VMEM] * (3 + len(arrivals)) + [ANY] * len(mark),
        out_specs=(VMEM,) * len(out_shape),
        scratch_shapes=[
            pltpu.VMEM((max(1, len(arrivals)), TILES // 4, 4, QBLK), F32),
            pltpu.VMEM((TILES // 4, 4, QBLK), F32),
        ],
        compiler_params=params(),
        cost_estimate=pl.CostEstimate(
            flops=TILES * 12 * QBLK * DH, bytes_accessed=4 * 2**20, transcendentals=0
        ),
        name=f"merge{j}",
    )(info, table, back, *own_part, *[acc for _, acc in arrivals], *mark)


def token_kernel(*refs):
    sources, out_ref, held, sems = refs[:-3], refs[-3], refs[-2], refs[-1]
    loads = [
        pltpu.make_async_copy(a.at[0, 0:16, :], held.at[i], sems.at[i])
        for i, a in enumerate(sources)
    ]
    for load in loads:
        load.start()
    for load in loads:
        load.wait()
    out_ref[...] = sum(held[i].astype(F32) for i in range(len(sources)))


def token(arrays):
    n = len(arrays)
    return pl.pallas_call(
        token_kernel,
        out_shape=jax.ShapeDtypeStruct((16, DH), F32),
        in_specs=[ANY] * n,
        out_specs=VMEM,
        scratch_shapes=[pltpu.VMEM((n, 16, DH), BF), pltpu.SemaphoreType.DMA((n,))],
        compiler_params=params(),
        name="token",
    )(*arrays)


def ring(x, step, axis="z", size=NZ):
    return lax.ppermute(x, axis, [(i, (i + step) % size) for i in range(size)])


def after(x, *others):
    return lax.optimization_barrier((x,) + others)[0]


CHUNKS = ((0,), (1, 7), (2, 6), (3, 5), (4,))


def shards(queries, win_key, win_value, past_key, past_value, chosen):
    x, z = lax.axis_index("x"), lax.axis_index("z")

    with jax.named_scope("prepare"):
        tiles = queries.reshape(TILES, QBLK, DH).swapaxes(1, 2)
        mine = jnp.pad(chosen.reshape(1, REQ), ((0, 0), (0, 128 - REQ)), constant_values=-4)

    with jax.named_scope("column"):
        away = (z + jnp.arange(NZ, dtype=jnp.int32)) % NZ
        column = lax.all_to_all(jnp.broadcast_to(mine, (NZ, 128)), "z", 0, 0, tiled=True)
    right = left = tiles
    sources = [(tiles,)]
    for step in range(1, 4):
        with jax.named_scope(f"ring{step}"):
            right, left = ring(right, 1), ring(left, -1)
        sources.append((left, right))
    with jax.named_scope("ring4"):
        sources.append((jnp.concatenate([ring(right[:16], 1), ring(left[16:], -1)], axis=0),))

    def coded(lists):
        plane_ids = jnp.arange(PLANE, dtype=jnp.int32)
        owner_ids = (plane_ids // 4) * 32 + (plane_ids % 4) * 8 + z
        entry = jnp.arange(128, dtype=jnp.int32) // TOPK * 4 + lists % 4 + 1
        found = jnp.where((lists // 4)[None] == owner_ids[:, None, None], entry[None], 0)
        return jnp.sum(found, axis=2)

    def tiles_in(code):
        return (jnp.maximum(code - 1, 0) // 4).reshape(-1)

    with jax.named_scope("lists"):
        tile_of_mine = tiles_in(coded(mine))
        column = jnp.take(column, away, axis=0)
        owner = column // 4
        code = coded(column)
        group = 2 * x + away // 4
        meta = jnp.where(code > 0, (code - 1) % 4 * 8 + group[None], -1)
        meta = jnp.pad(meta, ((0, 0), (0, 128 - NZ)))
        tile_of = tiles_in(code)
        place = (owner // 32) * 4 + owner % 32 // 8
        table = jnp.where(jnp.logical_and(owner % 8 == z, owner >= 0), place, -1).reshape(-1)
        info = jnp.where(jnp.arange(128, dtype=jnp.int32) == 0, z, x)
        meta, table, tile_of, info = lax.optimization_barrier((meta, table, tile_of, info))

    with jax.named_scope("kv"):
        own_k = win_key.reshape(QBLK, 4, 2, DH).transpose(1, 2, 0, 3)
        own_v = win_value.reshape(QBLK, 4, 2, DH).transpose(1, 2, 3, 0)
        pieces = jnp.concatenate([own_k, own_v], axis=1)
        kv = [lax.dynamic_index_in_dim(pieces, x, axis=0, keepdims=False)]
        for d in range(1, 4):
            piece = lax.dynamic_index_in_dim(pieces, (x + d) % 4, axis=0, keepdims=False)
            kv.append(ring(piece, d, "x", 4))
        kv = jnp.stack(kv)
        past_value_t = past_value.T

    previous = []

    def exchange(send, *others):
        send = after(send, *previous, *others)
        got = lax.all_to_all(send, ("y", "c", "x"), 0, 0, tiled=True)
        previous[:] = [got]
        return got

    def forward(chunks, *others):
        refs = [t for c in chunks for t in sources[c]]
        aways = [d for c in chunks for d in CHUNKS[c]]
        return exchange(pack(refs, aways, tile_of), *others)

    def partial(c, got, first=0):
        with jax.named_scope(f"far{c}"):
            return far(got, first, CHUNKS[c], meta, past_key, past_value_t)

    def own_part(c):
        with jax.named_scope(f"own{c}"):
            return tuple(own(sources[c], CHUNKS[c], kv, info))

    def merged(c, back, arrivals, spans=((0, 8),), mark=()):
        out = []
        with jax.named_scope(f"merge{c}"):
            for span in spans:
                for j, away_by in enumerate(CHUNKS[c]):
                    coming = [
                        (low, acc)
                        for (at, low, high), acc in arrivals
                        if at == j and low < span[1] and high > span[0]
                    ]
                    (acc,) = merge(j, away_by, info, table, back, owns[c], coming, (span,), mark)
                    out.append(((j,) + span, acc))
        return out

    def onward(c, parts):
        with jax.named_scope(f"return{c}"):
            return [(key, ring(acc, 1 - 2 * key[0])) for key, acc in parts]

    def arrays(arrivals):
        return [acc for _, acc in arrivals]

    with jax.named_scope("forward"):
        got0 = exchange(pack(sources[0], (0,), tile_of_mine), column, *sources[1])
        own0, own1 = own_part(0), own_part(1)
        meta = exchange(meta, past_value_t, *own0, *own1)[:, :NZ].reshape(-1)
        got12 = forward((1, 2))
        part0, own2 = partial(0, got0), own_part(2)
        got34 = forward((3, 4), part0, *own2)
        part2, own3, own4 = partial(2, got12, 2), own_part(3), own_part(4)
        part4 = partial(4, after(got34, part2, *own3, *own4), 2)
        part3, part1 = partial(3, got34), partial(1, got12)
    owns = [own0, own1, own2, own3, own4]
    with jax.named_scope("back"):
        back4 = exchange(part4)
        back3 = exchange(part3)
        (low, high) = merged(4, back4, [], ((0, 4), (4, 8)))
        arrivals = onward(4, [((0, 0, 4), low[1]), ((1, 4, 8), high[1])])
        back2 = exchange(part2, part1, *arrays(arrivals))
        arrivals = onward(3, merged(3, back3, arrivals))
        send1, mark = lax.optimization_barrier((part1, token(arrays(arrivals))))
        back1 = exchange(send1)
        arrivals = onward(2, merged(2, back2, arrivals, mark=(mark,)))
        back0 = exchange(part0)
        arrivals = onward(1, merged(1, back1, arrivals))
        arrivals = [(low, acc) for (_, low, _), acc in arrivals]
        return merge(0, 0, info, table, back0, own0, arrivals, None)[0]


def solution(mesh):
    inner = Mesh(mesh.devices.reshape(4, 2, 4, 8), ("y", "c", "x", "z"))
    rows, heads = ("y", "c"), ("x", "z")
    return jax.shard_map(
        shards,
        mesh=inner,
        in_specs=(
            P(rows, heads),
            P(rows + heads, None),
            P(rows + heads, None),
            P(rows + heads, None),
            P(rows + heads, None),
            P(rows, heads, None),
        ),
        out_specs=P(rows, heads),
        check_vma=False,
    )
```
